32 devices in a mesh: grp: 8 (over y, x, core), cache: 4 (over z).
Axes of the slice: x: 2, y: 2, z: 4, core: 2. Of those that a mesh axis runs over, the one named last changes fastest.
Arguments:
- tokens: bfloat16 [1536, 2048], P(('grp', 'cache')), may hold values from -6 to 6
- attn_gain: bfloat16 [2048], replicated, may hold values from 0.25 to 1.75
- w_query: bfloat16 [2048, 2048], P(None, 'cache'), may hold values from -0.125 to 0.125
- w_key: bfloat16 [2048, 512], P(None, 'cache'), may hold values from -0.125 to 0.125
- w_value: bfloat16 [2048, 512], P(None, 'cache'), may hold values from -0.125 to 0.125
- w_out: bfloat16 [2048, 2048], P('cache'), may hold values from -0.125 to 0.125
- mlp_gain: bfloat16 [2048], replicated, may hold values from 0.25 to 1.75
- w_gate: bfloat16 [2048, 8192], P(None, 'grp'), may hold values from -0.125 to 0.125
- w_up: bfloat16 [2048, 8192], P(None, 'grp'), may hold values from -0.125 to 0.125
- w_down: bfloat16 [8192, 2048], P('grp'), may hold values from -0.0625 to 0.0625
- key_cache: bfloat16 [24, 8, 4096, 64], P('grp', 'cache'), may hold values from -6 to 6
- value_cache: bfloat16 [24, 8, 4096, 64], P('grp', 'cache'), may hold values from -6 to 6
- lengths: int32 [24], P('grp'), may hold values from 1 to 4032, as said below
- parents: int32 [24, 64], P('grp'), may hold values from 0 to 62, as said below
- accepted: int32 [24, 8], P('grp'), may hold values from 0 to 63
Outputs:
- hidden: bfloat16 [1536, 2048], P(('grp', 'cache'))
- new_key_cache: bfloat16 [24, 8, 4096, 64], P('grp', 'cache')
- new_value_cache: bfloat16 [24, 8, 4096, 64], P('grp', 'cache')
The draws below stay inside these ranges and needn't reach their ends.
Inputs may be any that keep to these rules, and one draw needn't show every extreme that they name: `parents`: node 0 of each tree is its root with entry 0; every other node i has a parent below i. `lengths`: some request has exactly 4032 filled slots.
All inputs are finite; a program needn't handle non-finite values.
Results may differ from the reference program's by a relative error of at most 0.011.
Values may be sent and summed in bfloat16 or wider, within the bound.
A program may use at most 128 MiB of HBM per device.

```python
import jax
import jax.numpy as jnp
from jax import lax

D = 2048
HQ = 32
KVH = 8
HD = 64
FF = 8192
LEN = 4096
TREE = 64
ACC = 8
REQS = 24
TOKENS = 1536


def draw_parents(key, part):
    nodes = jnp.arange(TREE, dtype=jnp.int32)
    upper = jnp.maximum(nodes, 1)
    return jax.random.randint(key, (REQS, TREE), 0, upper[None, :]).astype(jnp.int32)


def draw_lengths(key, part):
    raw = jax.random.randint(key, (REQS,), 1, LEN - TREE + 1).astype(jnp.int32)
    return raw.at[0].set(LEN - TREE)


def set_ends(array, key, least, high):
    place = [jax.random.randint(jax.random.fold_in(key, axis), (), 0, length) for axis, length in enumerate(array.shape)]
    widest = array.shape.index(max(array.shape))
    neighbour = place[:widest] + [(place[widest] + 1) % array.shape[widest]] + place[widest + 1:]
    return array.at[tuple(place)].set(least).at[tuple(neighbour)].set(high)


def block_levels(stream_key, extent, shards, least, high):
    level, own = 1.0, jax.random.fold_in(stream_key, 6)
    for dim, shards_of in shards:
        draws = jnp.exp(jax.random.uniform(jax.random.fold_in(own, dim), (shards_of,), jnp.float32, least / len(shards), high / len(shards)))
        level = level * jnp.repeat(draws, extent[dim] // shards_of).reshape([-1 if axis == dim else 1 for axis in range(len(extent))])
    return level


def scatter_about(stream_key, shape, width, bound, shards=(), kind=jnp.bfloat16):
    values = jax.random.normal(stream_key, shape, jnp.float32) * width
    if len(shards) > 0:
        values = block_levels(stream_key, shape, shards, -0.22, 0.18) * values
    return jnp.clip(values, min=-bound, max=bound).astype(kind)


def setup_inputs(seed: int = 0) -> dict:
    streams_of = jax.random.split(jax.random.key(seed), 16)
    return {
        "tokens": scatter_about(streams_of[0], (TOKENS, D), 1.0, 6.0, ((0, 32),)),
        "attn_gain": jnp.clip(1.0 + 0.15 * jax.random.normal(streams_of[1], (D,), jnp.float32), 0.25, 1.75).astype(jnp.bfloat16),
        "w_query": scatter_about(streams_of[2], (D, HQ * HD), D ** -0.5, 0.125, ((1, 4),)),
        "w_key": scatter_about(streams_of[3], (D, KVH * HD), D ** -0.5, 0.125, ((1, 4),)),
        "w_value": scatter_about(streams_of[4], (D, KVH * HD), D ** -0.5, 0.125, ((1, 4),)),
        "w_out": scatter_about(streams_of[5], (HQ * HD, D), (HQ * HD) ** -0.5, 0.125, ((0, 4),)),
        "mlp_gain": jnp.clip(1.0 + 0.15 * jax.random.normal(streams_of[6], (D,), jnp.float32), 0.25, 1.75).astype(jnp.bfloat16),
        "w_gate": scatter_about(streams_of[7], (D, FF), D ** -0.5, 0.125, ((1, 8),)),
        "w_up": scatter_about(streams_of[8], (D, FF), D ** -0.5, 0.125, ((1, 8),)),
        "w_down": scatter_about(streams_of[9], (FF, D), FF ** -0.5, 0.0625, ((0, 8),)),
        "key_cache": scatter_about(streams_of[10], (REQS, KVH, LEN, HD), 1.0, 6.0, ((0, 8), (1, 4))),
        "value_cache": scatter_about(streams_of[11], (REQS, KVH, LEN, HD), 1.0, 6.0, ((0, 8), (1, 4))),
        "lengths": draw_lengths(jax.random.fold_in(streams_of[15], 71), 0),
        "parents": draw_parents(jax.random.fold_in(streams_of[15], 71), 0),
        "accepted": set_ends(jax.random.randint(streams_of[14], (REQS, ACC), 0, TREE), jax.random.fold_in(streams_of[14], 1), 0, TREE - 1).astype(jnp.int32),
    }


THETA = 10000.0

def ancestry(parent_row):
    count = parent_row.shape[0]
    nodes = jnp.arange(count, dtype=jnp.int32)
    linked = ((parent_row[:, None] == nodes[None, :]) & (nodes[:, None] > 0)).astype(jnp.float32)
    closure = jnp.eye(count, dtype=jnp.float32) + linked
    for sweep in range(count.bit_length()):
        closure = jnp.minimum(jnp.dot(closure, closure, precision=lax.Precision.HIGHEST), 1.0)
    depth = lax.optimization_barrier(jnp.sum(closure, axis=1)) - 1.0
    return (closure > 0.5, depth)

def rms_norm(values, gain):
    wide = values.astype(jnp.float32)
    scale = lax.rsqrt(lax.optimization_barrier(jnp.mean(wide * wide, axis=-1, keepdims=True)) + 1e-05)
    return (wide * scale * gain.astype(jnp.float32)).astype(jnp.bfloat16)

def rotate(values, where_at, head_dim):
    rows = values.shape[0]
    half = head_dim // 2
    shaped = values.reshape(rows, -1, head_dim)
    freq = jnp.power(jnp.float32(THETA), -jnp.arange(half, dtype=jnp.float32) * 2.0 / head_dim)
    angle = where_at[:, None] * freq[None, :]
    cosine = jnp.cos(angle)[:, None, :]
    sine = jnp.sin(angle)[:, None, :]
    first = shaped[..., :half]
    second = shaped[..., half:]
    turned = jnp.concatenate([first * cosine - second * sine, second * cosine + first * sine], axis=-1)
    return turned.reshape(rows, -1)

def attend(query, keys_old, values_old, keys_new, values_new, length, tree_mask):
    scale = 1.0 / jnp.sqrt(jnp.float32(query.shape[-1]))
    qf = query.astype(jnp.float32)
    cache_scores = jnp.einsum('tkgd,kld->kgtl', qf, keys_old.astype(jnp.float32)) * scale
    filled = jnp.arange(keys_old.shape[1], dtype=jnp.int32) < length
    cache_exp = jnp.where(filled[None, None, None, :], jnp.exp(cache_scores), 0.0)
    tree_scores = jnp.einsum('tkgd,ukd->kgtu', qf, keys_new.astype(jnp.float32)) * scale
    tree_exp = jnp.where(tree_mask[None, None], jnp.exp(tree_scores), 0.0)
    denom = lax.optimization_barrier(jnp.sum(cache_exp, axis=-1)) + lax.optimization_barrier(jnp.sum(tree_exp, axis=-1))
    cache_probs = (cache_exp / denom[..., None]).astype(jnp.bfloat16)
    tree_probs = (tree_exp / denom[..., None]).astype(jnp.bfloat16)
    result = jnp.einsum('kgtl,kld->tkgd', cache_probs.astype(jnp.float32), values_old.astype(jnp.float32))
    result = result + jnp.einsum('kgtu,ukd->tkgd', tree_probs.astype(jnp.float32), values_new.astype(jnp.float32))
    return result.astype(jnp.bfloat16).reshape(query.shape[0], -1)

def compact(cache_block, tree_rows, picks, length):
    chosen = jnp.transpose(tree_rows[picks], (1, 0, 2))
    zero = jnp.zeros((), jnp.int32)
    return lax.dynamic_update_slice(cache_block, chosen, (zero, length.astype(jnp.int32), zero))

def reference(tokens, attn_gain, w_query, w_key, w_value, w_out, mlp_gain, w_gate, w_up, w_down, key_cache, value_cache, lengths, parents, accepted):
    masks, depths = jax.vmap(ancestry)(parents)
    positions = (lengths[:, None].astype(jnp.float32) + depths).reshape(-1)
    normed = rms_norm(tokens, attn_gain)
    query = rotate(jnp.dot(normed, w_query, preferred_element_type=jnp.float32), positions, HD).astype(jnp.bfloat16)
    key_tree = rotate(jnp.dot(normed, w_key, preferred_element_type=jnp.float32), positions, HD).astype(jnp.bfloat16)
    value_tree = jnp.dot(normed, w_value, preferred_element_type=jnp.float32).astype(jnp.bfloat16)
    query = query.reshape(REQS, TREE, KVH, HQ // KVH, HD)
    key_tree = key_tree.reshape(REQS, TREE, KVH, HD)
    value_tree = value_tree.reshape(REQS, TREE, KVH, HD)

    def per_request(items):
        query_r, keys_old, values_old, keys_new, values_new, length, tree_mask, picks = items
        result = attend(query_r, keys_old, values_old, keys_new, values_new, length, tree_mask)
        return (result, compact(keys_old, keys_new, picks, length), compact(values_old, values_new, picks, length))
    attended, new_keys, new_values = lax.map(per_request, (query, key_cache, value_cache, key_tree, value_tree, lengths, masks, accepted))
    attended = attended.reshape(TOKENS, HQ * HD)
    mixed = (tokens.astype(jnp.float32) + jnp.dot(attended, w_out, preferred_element_type=jnp.float32)).astype(jnp.bfloat16)
    normed_two = rms_norm(mixed, mlp_gain)
    gate = jnp.dot(normed_two, w_gate, preferred_element_type=jnp.float32)
    upper = jnp.dot(normed_two, w_up, preferred_element_type=jnp.float32)
    units = (jax.nn.silu(gate) * upper).astype(jnp.bfloat16)
    hidden = (mixed.astype(jnp.float32) + jnp.dot(units, w_down, preferred_element_type=jnp.float32)).astype(jnp.bfloat16)
    return (hidden, new_keys, new_values)
```

```python
import functools

import jax
import jax.numpy as jnp
from jax import lax
from jax.experimental import pallas as pl
from jax.experimental.pallas import tpu as pltpu
from jax.sharding import PartitionSpec as P

THETA = 10000.0
MESH = pl.DeviceIdType.MESH
F32 = jnp.float32
BF16 = jnp.bfloat16


def ancestry(parent_row):
    count = parent_row.shape[0]
    nodes = jnp.arange(count, dtype=jnp.int32)
    linked = ((parent_row[:, None] == nodes[None, :]) & (nodes[:, None] > 0)).astype(F32)
    closure = jnp.eye(count, dtype=F32) + linked
    for sweep in range((count - 1).bit_length()):
        half = closure.astype(BF16)
        closure = jnp.minimum(jnp.dot(half, half, preferred_element_type=F32), 1.0)
    depth = jnp.sum(closure, axis=1) - 1.0
    return (closure, depth)


def norm(wide, gain):
    scale = lax.rsqrt(jnp.mean(wide * wide, axis=-1, keepdims=True) + 1e-05)
    return (wide * scale * gain.astype(F32)).astype(BF16)


def turn(values, cosine, sine, head_dim):
    width = values.shape[1]
    half = head_dim // 2
    if width % 128 == 0:
        lane = lax.broadcasted_iota(jnp.int32, values.shape, 1)
        other = jnp.where(
            lane % head_dim < half,
            pltpu.roll(values, width - half, 1),
            pltpu.roll(values, half, 1),
        )
        times = width // cosine.shape[1]
        cosine = jnp.concatenate([cosine] * times, axis=1)
        sine = jnp.concatenate([sine] * times, axis=1)
    else:
        parts = []
        for at in range(0, width, head_dim):
            parts += [values[:, at + half : at + head_dim], values[:, at : at + half]]
        other = jnp.concatenate(parts, axis=1)
        cosine, sine = cosine[:, :width], sine[:, :width]
    return values * cosine + other * sine


def project_kernel(
    n, head_dim, tokens, gain, cosine, sine, wq, wk, wv, q_out, k_out, v_out,
    held, wq_v, wk_v, wv_v, w_sem, left_send, left_recv, right_send, right_recv,
):
    me = lax.axis_index("cache")
    barrier = pltpu.get_barrier_semaphore()
    for step in range(1, n):
        pl.semaphore_signal(
            barrier, inc=1, device_id={"cache": lax.rem(me + step, n)}, device_id_type=MESH
        )
    loads = [
        pltpu.make_async_copy(src, dst, w_sem.at[i])
        for i, (src, dst) in enumerate(((wq, wq_v), (wk, wk_v), (wv, wv_v)))
    ]
    for load in loads:
        load.start()
    held[me] = norm(tokens[...].astype(F32), gain[...])
    pl.semaphore_wait(barrier, n - 1)

    def to_right(block):
        return pltpu.make_async_remote_copy(
            held.at[block], held.at[block], right_send.at[block], right_recv.at[block],
            device_id={"cache": lax.rem(me + 1, n)}, device_id_type=MESH,
        )

    def to_left(block):
        return pltpu.make_async_remote_copy(
            held.at[block], held.at[block], left_send.at[block], left_recv.at[block],
            device_id={"cache": lax.rem(me + n - 1, n)}, device_id_type=MESH,
        )

    def compute(block):
        x = held[block]
        cos, sin = cosine[block], sine[block]
        q_out[block] = turn(
            jnp.dot(x, wq_v[...], preferred_element_type=F32), cos, sin, head_dim
        ).astype(BF16)
        k_out[block] = turn(
            jnp.dot(x, wk_v[...], preferred_element_type=F32), cos, sin, head_dim
        ).astype(BF16)
        v_out[block] = jnp.dot(x, wv_v[...], preferred_element_type=F32).astype(BF16)

    @pl.when(me < n - 1)
    def _():
        to_right(me).start()

    @pl.when(me > 0)
    def _():
        to_left(me).start()

    for load in loads:
        load.wait()
    compute(me)

    def hop(step, carry):
        low, high = me - step, me + step

        @pl.when(low >= 0)
        def _():
            to_right(low).wait_recv()

            @pl.when(me < n - 1)
            def _():
                to_right(low).start()

        @pl.when(high < n)
        def _():
            to_left(high).wait_recv()

            @pl.when(me > 0)
            def _():
                to_left(high).start()

        @pl.when(low >= 0)
        def _():
            compute(low)

        @pl.when(high < n)
        def _():
            compute(high)

        return carry

    lax.fori_loop(1, n, hop, 0)

    for block in range(n):
        @pl.when((block <= me) & (me < n - 1))
        def _():
            to_right(block).wait_send()

        @pl.when((block >= me) & (me > 0))
        def _():
            to_left(block).wait_send()


def attend_kernel(
    heads, head_dim, chunk, lengths, accepted, q_ref, k_ref, v_ref, mask_ref, kc, vc,
    o_ref, kc_out, vc_out,
):
    request = pl.program_id(0)
    length = lengths[request]
    slots = kc.shape[3]
    tree = q_ref.shape[0]
    group = q_ref.shape[1] // (heads * head_dim)
    factor = (head_dim ** -0.5) * 1.4426950408889634
    picks = accepted.shape[1]
    window = 256
    base = pl.multiple_of(jnp.minimum((length // 128) * 128, slots - window), 128)
    node = lax.broadcasted_iota(jnp.int32, (tree, window), 0)
    slot = lax.broadcasted_iota(jnp.int32, (tree, window), 1) + base - length
    chosen = jnp.zeros((tree, window), F32)
    for j in range(picks):
        hit = (slot == j) & (node == accepted[request, j])
        chosen = jnp.where(hit, 1.0, chosen)
    chosen = chosen.astype(BF16)
    slot_h = lax.broadcasted_iota(jnp.int32, (head_dim, window), 1) + base - length
    fresh = (slot_h >= 0) & (slot_h < picks)
    mask = jnp.concatenate([mask_ref[...]] * group, axis=0) > 0.5
    trans = (((1,), (1,)), ((), ()))
    first = (((0,), (0,)), ((), ()))

    for head in range(heads):
        at = head * group * head_dim
        query = jnp.concatenate(
            [q_ref[:, at + g * head_dim : at + (g + 1) * head_dim] for g in range(group)], axis=0
        )
        k_new = k_ref[:, head * head_dim : (head + 1) * head_dim]
        v_new = v_ref[:, head * head_dim : (head + 1) * head_dim]
        scores = lax.dot_general(query, k_new, trans, preferred_element_type=F32) * factor
        scores = jnp.where(mask, scores, -jnp.inf)
        top = jnp.max(scores, axis=1, keepdims=True)
        exps = jnp.exp2(scores - top)
        total = jnp.sum(exps, axis=1, keepdims=True)
        mix = jnp.dot(exps.astype(BF16), v_new, preferred_element_type=F32)

        def part(i, carry):
            top, total, mix = carry
            start = pl.multiple_of(i * chunk, chunk)
            keys = kc[0, head, :, pl.ds(start, chunk)]
            values = vc[0, head, :, pl.ds(start, chunk)]
            scores = jnp.dot(query, keys, preferred_element_type=F32) * factor
            where_at = lax.broadcasted_iota(jnp.int32, (1, chunk), 1) + start
            scores = scores + jnp.where(where_at < length, 0.0, -jnp.inf)
            high = jnp.maximum(top, jnp.max(scores, axis=1, keepdims=True))
            shrink = jnp.exp2(top - high)
            exps = jnp.exp2(scores - high)
            total = total * shrink + jnp.sum(exps, axis=1, keepdims=True)
            mix = mix * shrink + lax.dot_general(
                exps.astype(BF16), values, trans, preferred_element_type=F32
            )
            return high, total, mix

        top, total, mix = lax.fori_loop(0, (length + chunk - 1) // chunk, part, (top, total, mix))
        out = (mix / total).astype(BF16)
        for g in range(group):
            o_ref[:, at + g * head_dim : at + (g + 1) * head_dim] = out[g * tree : (g + 1) * tree]

        for cache, new, result in ((kc, k_new, kc_out), (vc, v_new, vc_out)):
            result[0, head] = cache[0, head]
            placed = lax.dot_general(new, chosen, first, preferred_element_type=F32).astype(BF16)
            old = cache[0, head, :, pl.ds(base, window)]
            result[0, head, :, pl.ds(base, window)] = jnp.where(fresh, placed, old)


def finish_kernel(
    n, chips, att, tokens, gain, wo, wg, wu, wd, out,
    wo_v, wg_v, wu_v, wd_v, part, from_left, from_right, right_out, left_out,
    mixed, xg, units, dpart, sib_in, fin_out, fin_in,
    w_sem, r_send, r_recv, l_send, l_recv, a_send, a_recv, f_send, f_recv,
    s_send, s_recv, e_send, e_recv,
):
    me = lax.axis_index("cache")
    grp = lax.axis_index("grp")
    chip, core = grp // 2, lax.rem(grp, 2)
    sibling = {"grp": chip * 2 + 1 - core}
    rows, depth = tokens.shape

    def chip_at(step):
        return {"grp": lax.rem(chip + step + chips, chips) * 2 + core}

    barrier = pltpu.get_barrier_semaphore()
    for step in range(1, n):
        pl.semaphore_signal(
            barrier, inc=1, device_id={"cache": lax.rem(me + step, n)}, device_id_type=MESH
        )
    pl.semaphore_signal(barrier, inc=1, device_id=sibling, device_id_type=MESH)
    for step in range(1, chips):
        pl.semaphore_signal(barrier, inc=1, device_id=chip_at(step), device_id_type=MESH)
    loads = [
        pltpu.make_async_copy(src, dst, w_sem.at[i])
        for i, (src, dst) in enumerate(((wo, wo_v), (wg, wg_v), (wu, wu_v), (wd, wd_v)))
    ]
    for load in loads:
        load.start()

    @pl.when(me == 0)
    def _():
        from_left[...] = jnp.zeros_like(from_left)

    @pl.when(me == n - 1)
    def _():
        from_right[...] = jnp.zeros_like(from_right)

    loads[0].wait()
    pl.semaphore_wait(barrier, n - 1 + 1 + chips - 1)

    def right_copy(block):
        return pltpu.make_async_remote_copy(
            right_out.at[block], from_left.at[block], r_send.at[block], r_recv.at[block],
            device_id={"cache": lax.rem(me + 1, n)}, device_id_type=MESH,
        )

    def left_copy(block):
        return pltpu.make_async_remote_copy(
            left_out.at[block], from_right.at[block], l_send.at[block], l_recv.at[block],
            device_id={"cache": lax.rem(me + n - 1, n)}, device_id_type=MESH,
        )

    def push_right(block):
        @pl.when(me < block)
        def _():
            @pl.when(me > 0)
            def _():
                right_copy(block).wait_recv()

            right_out[block] = (part[block] + from_left[block].astype(F32)).astype(BF16)
            right_copy(block).start()

    def push_left(block):
        @pl.when(me > block)
        def _():
            @pl.when(me < n - 1)
            def _():
                left_copy(block).wait_recv()

            left_out[block] = (part[block] + from_right[block].astype(F32)).astype(BF16)
            left_copy(block).start()

    done = set()
    for step in range(n):
        for block in (n - 1 - step, step):
            if block not in done:
                done.add(block)
                part[block] = jnp.dot(att[block], wo_v[...], preferred_element_type=F32)
        if step == n - 1:
            break

        @pl.when(me < n // 2)
        def _():
            push_right(n - 1 - step)

        push_left(step)

        @pl.when(me >= n // 2)
        def _():
            push_right(n - 1 - step)

    @pl.when(me > 0)
    def _():
        right_copy(me).wait_recv()

    @pl.when(me < n - 1)
    def _():
        left_copy(me).wait_recv()

    whole = part[me] + from_left[me].astype(F32) + from_right[me].astype(F32)
    mixed[...] = (tokens[...].astype(F32) + whole).astype(BF16)
    xg[0] = norm(mixed[...].astype(F32), gain[...])

    def gather_copy(j):
        return pltpu.make_async_remote_copy(
            xg.at[0], xg.at[2 * j], a_send.at[j], a_recv.at[j],
            device_id=chip_at(j), device_id_type=MESH,
        )

    def pass_copy(j):
        return pltpu.make_async_remote_copy(
            xg.at[2 * j], xg.at[2 * j + 1], f_send.at[j], f_recv.at[j],
            device_id=sibling, device_id_type=MESH,
        )

    for j in range(1, chips):
        gather_copy(j).start()
    pass_copy(0).start()
    for j in range(1, chips):
        gather_copy(j).wait_recv()
        pass_copy(j).start()
    for j in range(chips):
        pass_copy(j).wait_recv()
    loads[1].wait()
    loads[2].wait()

    if rows % 16 == 0:
        x = xg[...].reshape(2 * chips * rows, depth)
    else:
        x = xg[...].astype(F32).reshape(2 * chips * rows, depth).astype(BF16)
    wide = 256

    def gate_tile(i, carry):
        at = pl.ds(pl.multiple_of(i * wide, wide), wide)
        gate = jnp.dot(x, wg_v[:, at], preferred_element_type=F32)
        upper = jnp.dot(x, wu_v[:, at], preferred_element_type=F32)
        unit = gate / (1.0 + jnp.exp(-gate)) * upper
        units[:, :, at] = unit.astype(BF16).reshape(chips, 2 * rows, wide)
        return carry

    lax.fori_loop(0, wg_v.shape[1] // wide, gate_tile, 0)
    loads[3].wait()
    tall = 512

    def down(j):
        u = units[j]

        def tile(i, carry):
            at = pl.ds(pl.multiple_of(i * tall, tall), tall)
            y = jnp.dot(u, wd_v[:, at], preferred_element_type=F32)
            dpart[2 * j, :, at] = y[:rows].astype(BF16)
            dpart[2 * j + 1, :, at] = y[rows:].astype(BF16)
            return carry

        lax.fori_loop(0, depth // tall, tile, 0)

    def sib_copy(j):
        return pltpu.make_async_remote_copy(
            dpart.at[2 * j + 1], sib_in.at[j], s_send.at[j], s_recv.at[j],
            device_id=sibling, device_id_type=MESH,
        )

    def end_copy(j):
        return pltpu.make_async_remote_copy(
            fin_out.at[j], fin_in.at[j], e_send.at[j], e_recv.at[j],
            device_id=chip_at(-j), device_id_type=MESH,
        )

    def send_on(j):
        sib_copy(j).wait_recv()
        fin_out[j] = (dpart[2 * j].astype(F32) + sib_in[j].astype(F32)).astype(BF16)
        end_copy(j).start()

    for j in range(1, chips):
        down(j)
        sib_copy(j).start()
        if j > 1:
            send_on(j - 1)
    down(0)
    sib_copy(0).start()
    if chips > 1:
        send_on(chips - 1)
    sib_copy(0).wait_recv()
    total = mixed[...].astype(F32) + dpart[0].astype(F32) + sib_in[0].astype(F32)
    for j in range(1, chips):
        end_copy(j).wait_recv()
        total = total + fin_in[j].astype(F32)
    out[...] = total.astype(BF16)

    for block in range(n):
        @pl.when(me < block)
        def _():
            right_copy(block).wait_send()

        @pl.when(me > block)
        def _():
            left_copy(block).wait_send()

    for j in range(chips):
        if j > 0:
            gather_copy(j).wait_send()
            end_copy(j).wait_send()
        pass_copy(j).wait_send()
        sib_copy(j).wait_send()


def on_device(
    n, groups, tokens, attn_gain, w_query, w_key, w_value, w_out, mlp_gain, w_gate, w_up, w_down,
    key_cache, value_cache, lengths, parents, accepted,
):
    requests, heads, slots, head_dim = key_cache.shape
    tree = parents.shape[1]
    rows, depth = tokens.shape
    q_width, kv_width, ff = w_query.shape[1], w_key.shape[1], w_gate.shape[1]
    chips = groups // 2
    masks, depths = jax.vmap(ancestry)(parents)
    positions = (lengths[:, None].astype(F32) + depths).reshape(-1)
    half = head_dim // 2
    freq = jnp.power(F32(THETA), -jnp.arange(half, dtype=F32) * 2.0 / head_dim)
    angle = positions[:, None] * freq[None, :]
    cosine, sine = jnp.cos(angle), jnp.sin(angle)
    cosine = jnp.concatenate([cosine] * 4, axis=1).reshape(n, rows, 2 * head_dim)
    sine = jnp.concatenate([-sine, sine] * 2, axis=1).reshape(n, rows, 2 * head_dim)

    vmem = pl.BlockSpec(memory_space=pltpu.VMEM)
    hbm = pl.BlockSpec(memory_space=pl.ANY)
    dma = pltpu.SemaphoreType.DMA
    query, keys, values = pl.pallas_call(
        functools.partial(project_kernel, n, head_dim),
        out_shape=[
            jax.ShapeDtypeStruct((n, rows, width), BF16) for width in (q_width, kv_width, kv_width)
        ],
        in_specs=[vmem] * 4 + [hbm] * 3,
        out_specs=[vmem] * 3,
        scratch_shapes=[
            pltpu.VMEM((n, rows, depth), BF16),
            pltpu.VMEM(w_query.shape, BF16),
            pltpu.VMEM(w_key.shape, BF16),
            pltpu.VMEM(w_value.shape, BF16),
            dma((3,)), dma((n,)), dma((n,)), dma((n,)), dma((n,)),
        ],
        compiler_params=pltpu.CompilerParams(
            collective_id=0, has_side_effects=True, vmem_limit_bytes=32 * 2**20
        ),
        name="project",
    )(tokens, attn_gain.reshape(1, -1), cosine, sine, w_query, w_key, w_value)

    chunk = 1024
    cache_spec = pl.BlockSpec((1, heads, head_dim, slots), lambda r, *_: (r, 0, 0, 0))
    flipped = jax.ShapeDtypeStruct((requests, heads, head_dim, slots), BF16)

    def rows_spec(width):
        return pl.BlockSpec((tree, width), lambda r, *_: (r, 0))

    attended, new_keys, new_values = pl.pallas_call(
        functools.partial(attend_kernel, heads, head_dim, chunk),
        out_shape=[jax.ShapeDtypeStruct((requests * tree, q_width), BF16), flipped, flipped],
        grid_spec=pltpu.PrefetchScalarGridSpec(
            num_scalar_prefetch=2,
            grid=(requests,),
            in_specs=[
                rows_spec(q_width), rows_spec(kv_width), rows_spec(kv_width), rows_spec(tree),
                cache_spec, cache_spec,
            ],
            out_specs=[rows_spec(q_width), cache_spec, cache_spec],
        ),
        compiler_params=pltpu.CompilerParams(vmem_limit_bytes=40 * 2**20),
        name="attend",
    )(
        lengths, accepted,
        query.reshape(-1, q_width), keys.reshape(-1, kv_width), values.reshape(-1, kv_width),
        masks.reshape(-1, tree),
        jnp.swapaxes(key_cache, 2, 3), jnp.swapaxes(value_cache, 2, 3),
    )

    def blocks(count):
        return pltpu.VMEM((count, rows, depth), BF16)

    hidden = pl.pallas_call(
        functools.partial(finish_kernel, n, chips),
        out_shape=jax.ShapeDtypeStruct((rows, depth), BF16),
        in_specs=[vmem] * 3 + [hbm] * 4,
        out_specs=vmem,
        scratch_shapes=[
            pltpu.VMEM(w_out.shape, BF16),
            pltpu.VMEM(w_gate.shape, BF16),
            pltpu.VMEM(w_up.shape, BF16),
            pltpu.VMEM(w_down.shape, BF16),
            pltpu.VMEM((n, rows, depth), F32),
            blocks(n), blocks(n), blocks(n), blocks(n),
            pltpu.VMEM((rows, depth), BF16),
            blocks(2 * chips),
            pltpu.VMEM((chips, 2 * rows, ff), BF16),
            blocks(2 * chips),
            blocks(chips), blocks(chips), blocks(chips),
            dma((4,)),
            dma((n,)), dma((n,)), dma((n,)), dma((n,)),
            dma((chips,)), dma((chips,)), dma((chips,)), dma((chips,)),
            dma((chips,)), dma((chips,)), dma((chips,)), dma((chips,)),
        ],
        compiler_params=pltpu.CompilerParams(
            collective_id=1, has_side_effects=True, vmem_limit_bytes=50 * 2**20
        ),
        name="finish",
    )(
        attended.reshape(n, rows, q_width), tokens, mlp_gain.reshape(1, -1),
        w_out, w_gate, w_up, w_down,
    )
    return (hidden, jnp.swapaxes(new_keys, 2, 3), jnp.swapaxes(new_values, 2, 3))


def solution(mesh):
    placed = (
        P(("grp", "cache"), None),
        P(),
        P(None, "cache"),
        P(None, "cache"),
        P(None, "cache"),
        P("cache", None),
        P(),
        P(None, "grp"),
        P(None, "grp"),
        P("grp", None),
        P("grp", "cache", None, None),
        P("grp", "cache", None, None),
        P("grp"),
        P("grp", None),
        P("grp", None),
    )
    return jax.shard_map(
        functools.partial(on_device, mesh.shape["cache"], mesh.shape["grp"]),
        mesh=mesh,
        in_specs=placed,
        out_specs=(
            P(("grp", "cache"), None),
            P("grp", "cache", None, None),
            P("grp", "cache", None, None),
        ),
        check_vma=False,
    )
```

```python
import functools

import jax
import jax.numpy as jnp
import numpy as np
from jax import lax
from jax.experimental import pallas as pl
from jax.experimental.pallas import tpu as pltpu
from jax.sharding import PartitionSpec as P

THETA = 10000.0
MESH = pl.DeviceIdType.MESH
F32 = jnp.float32
BF16 = jnp.bfloat16
VMEM_BYTES = 60 * 2**20


def family(parent_row, count):
    row = lax.broadcasted_iota(jnp.int32, (count, count), 0)
    lane = lax.broadcasted_iota(jnp.int32, (count, count), 1)
    linked = ((parent_row == row) & (lane > 0)) | (row == lane)
    flipped = jnp.where(linked, 1.0, 0.0).astype(BF16)
    for sweep in range((count - 1).bit_length()):
        flipped = jnp.minimum(
            jnp.dot(flipped, flipped, preferred_element_type=F32), 1.0
        ).astype(BF16)
    same = jnp.where(row == lane, 1.0, 0.0).astype(BF16)
    first = (((0,), (0,)), ((), ()))
    closure = lax.dot_general(flipped, same, first, preferred_element_type=F32)
    ones = jnp.ones((count, 128), BF16)
    depth = lax.dot_general(flipped, ones, first, preferred_element_type=F32) - 1.0
    return closure, depth


def norm(wide, gain):
    scale = lax.rsqrt(jnp.mean(wide * wide, axis=-1, keepdims=True) + 1e-05)
    return (wide * scale * gain.astype(F32)).astype(BF16)


def turn(values, cosine, sine, head_dim):
    width = values.shape[1]
    half = head_dim // 2
    if width % 128 == 0:
        lane = lax.broadcasted_iota(jnp.int32, values.shape, 1)
        other = jnp.where(
            lane % head_dim < half,
            pltpu.roll(values, width - half, 1),
            pltpu.roll(values, half, 1),
        )
        times = width // cosine.shape[1]
        cosine = jnp.concatenate([cosine] * times, axis=1)
        sine = jnp.concatenate([sine] * times, axis=1)
    else:
        parts = []
        for at in range(0, width, head_dim):
            parts += [values[:, at + half : at + head_dim], values[:, at : at + half]]
        other = jnp.concatenate(parts, axis=1)
        cosine, sine = cosine[:, :width], sine[:, :width]
    return values * cosine + other * sine


def project_kernel(
    n, head_dim, lengths, tokens, gain, parents, freq, wq, wk, wv, q_out, k_out, v_out, mask_out,
    cosine, sine, held, wq_v, wk_v, wv_v, w_sem, left_send, left_recv, right_send, right_recv,
):
    me = lax.axis_index("cache")
    barrier = pltpu.get_barrier_semaphore()
    for step in range(1, n):
        pl.semaphore_signal(
            barrier, inc=1, device_id={"cache": lax.rem(me + step, n)}, device_id_type=MESH
        )
    loads = [
        pltpu.make_async_copy(src, dst, w_sem.at[i])
        for i, (src, dst) in enumerate(((wq, wq_v), (wk, wk_v), (wv, wv_v)))
    ]
    for load in loads:
        load.start()
    held[me] = norm(tokens[...].astype(F32), gain[...])
    pl.semaphore_wait(barrier, n - 1)

    def to_right(block):
        return pltpu.make_async_remote_copy(
            held.at[block], held.at[block], right_send.at[block], right_recv.at[block],
            device_id={"cache": lax.rem(me + 1, n)}, device_id_type=MESH,
        )

    def to_left(block):
        return pltpu.make_async_remote_copy(
            held.at[block], held.at[block], left_send.at[block], left_recv.at[block],
            device_id={"cache": lax.rem(me + n - 1, n)}, device_id_type=MESH,
        )

    rows = tokens.shape[0]

    def compute(block):
        x = held[block]
        at = pl.ds(pl.multiple_of(block * rows, 8), rows)
        cos, sin = cosine[at, :], sine[at, :]
        q_out[block] = turn(
            jnp.dot(x, wq_v[...], preferred_element_type=F32), cos, sin, head_dim
        ).astype(BF16)
        k_out[block] = turn(
            jnp.dot(x, wk_v[...], preferred_element_type=F32), cos, sin, head_dim
        ).astype(BF16)
        v_out[block] = jnp.dot(x, wv_v[...], preferred_element_type=F32).astype(BF16)

    @pl.when(me < n - 1)
    def _():
        to_right(me).start()

    @pl.when(me > 0)
    def _():
        to_left(me).start()

    requests, tree = parents.shape
    lane = lax.broadcasted_iota(jnp.int32, (tree, 128), 1)
    for r in range(requests):
        at = slice(r * tree, (r + 1) * tree)
        mask_out[at, :], depth = family(parents[r : r + 1, :], tree)
        angle = (depth + lengths[r].astype(F32)) * freq[...]
        cosine[at, :] = jnp.cos(angle)
        flat = jnp.sin(angle)
        sine[at, :] = jnp.where(lane % head_dim < head_dim // 2, -flat, flat)
    for load in loads:
        load.wait()
    compute(me)

    def hop(step, carry):
        low, high = me - step, me + step

        @pl.when(low >= 0)
        def _():
            to_right(low).wait_recv()

            @pl.when(me < n - 1)
            def _():
                to_right(low).start()

        @pl.when(high < n)
        def _():
            to_left(high).wait_recv()

            @pl.when(me > 0)
            def _():
                to_left(high).start()

        @pl.when(low >= 0)
        def _():
            compute(low)

        @pl.when(high < n)
        def _():
            compute(high)

        return carry

    lax.fori_loop(1, n, hop, 0)

    for block in range(n):
        @pl.when((block <= me) & (me < n - 1))
        def _():
            to_right(block).wait_send()

        @pl.when((block >= me) & (me > 0))
        def _():
            to_left(block).wait_send()


def attend_kernel(
    heads, head_dim, chunk, lengths, accepted, q_ref, k_ref, v_ref, mask_ref, kc, vc,
    o_ref, kc_out, vc_out,
):
    request = pl.program_id(0)
    length = lengths[request]
    slots = kc.shape[3]
    tree = q_ref.shape[0]
    group = q_ref.shape[1] // (heads * head_dim)
    factor = (head_dim ** -0.5) * 1.4426950408889634
    picks = accepted.shape[1]
    window = 256
    base = pl.multiple_of(jnp.minimum((length // 128) * 128, slots - window), 128)
    node = lax.broadcasted_iota(jnp.int32, (tree, window), 0)
    slot = lax.broadcasted_iota(jnp.int32, (tree, window), 1) + base - length
    chosen = jnp.zeros((tree, window), F32)
    for j in range(picks):
        hit = (slot == j) & (node == accepted[request, j])
        chosen = jnp.where(hit, 1.0, chosen)
    chosen = chosen.astype(BF16)
    slot_h = lax.broadcasted_iota(jnp.int32, (head_dim, window), 1) + base - length
    fresh = (slot_h >= 0) & (slot_h < picks)
    mask = jnp.concatenate([mask_ref[...]] * group, axis=0) > 0.5
    trans = (((1,), (1,)), ((), ()))
    first = (((0,), (0,)), ((), ()))

    def join(scores, values, carry, dims):
        top, total, mix = carry
        high = jnp.maximum(top, jnp.max(scores, axis=1, keepdims=True))
        shrink = jnp.exp2((top - high) * factor)
        exps = jnp.exp2((scores - high) * factor)
        total = total * shrink + jnp.sum(exps, axis=1, keepdims=True)
        mix = mix * shrink + lax.dot_general(
            exps.astype(BF16), values, dims, preferred_element_type=F32
        )
        return high, total, mix

    plain = (((1,), (0,)), ((), ()))
    queries, states = [], []
    for head in range(heads):
        at = head * group * head_dim
        query = jnp.concatenate(
            [q_ref[:, at + g * head_dim : at + (g + 1) * head_dim] for g in range(group)], axis=0
        )
        k_new = k_ref[:, head * head_dim : (head + 1) * head_dim]
        v_new = v_ref[:, head * head_dim : (head + 1) * head_dim]
        scores = lax.dot_general(query, k_new, trans, preferred_element_type=F32)
        scores = jnp.where(mask, scores, -jnp.inf)
        top = jnp.max(scores, axis=1, keepdims=True)
        exps = jnp.exp2((scores - top) * factor)
        total = jnp.sum(exps, axis=1, keepdims=True)
        mix = lax.dot_general(exps.astype(BF16), v_new, plain, preferred_element_type=F32)
        queries.append(query)
        states.append((top, total, mix))

    def part(i, carry):
        at = pl.ds(pl.multiple_of(i * chunk, chunk), chunk)
        scores = [
            jnp.dot(queries[head], kc[0, head, :, at], preferred_element_type=F32)
            for head in range(heads)
        ]
        return tuple(
            join(scores[head], vc[0, head, :, at], carry[head], trans) for head in range(heads)
        )

    full = length // chunk
    states = lax.fori_loop(0, full, part, tuple(states))
    start = pl.multiple_of(jnp.minimum(full * chunk, slots - chunk), chunk)
    at = pl.ds(start, chunk)
    where_at = lax.broadcasted_iota(jnp.int32, (1, chunk), 1) + start
    valid = (where_at < length) & (where_at >= full * chunk)
    for head in range(heads):
        scores = jnp.dot(queries[head], kc[0, head, :, at], preferred_element_type=F32)
        scores = jnp.where(valid, scores, -jnp.inf)
        top, total, mix = join(scores, vc[0, head, :, at], states[head], trans)
        out = (mix / total).astype(BF16)
        base_at = head * group * head_dim
        for g in range(group):
            o_ref[:, base_at + g * head_dim : base_at + (g + 1) * head_dim] = out[
                g * tree : (g + 1) * tree
            ]

        for cache, fed, result in ((kc, k_ref, kc_out), (vc, v_ref, vc_out)):
            new = fed[:, head * head_dim : (head + 1) * head_dim]
            result[0, head] = cache[0, head]
            placed = lax.dot_general(new, chosen, first, preferred_element_type=F32).astype(BF16)
            old = cache[0, head, :, pl.ds(base, window)]
            result[0, head, :, pl.ds(base, window)] = jnp.where(fresh, placed, old)


def finish_kernel(
    n, chips, parts, att, tokens, gain, wo, wg, wu, wd, out,
    wo_v, wg_v, wu_v, wd_v, z_out, z_in, mixed, xg, units, dpart, sib_in, fin_out, fin_in,
    w_sem, z_send, z_recv, a_send, a_recv, f_send, f_recv, s_send, s_recv, e_send, e_recv,
):
    me = lax.axis_index("cache")
    grp = lax.axis_index("grp")
    chip, core = grp // 2, lax.rem(grp, 2)
    sibling = {"grp": chip * 2 + 1 - core}
    rows, depth = tokens.shape
    sub = rows // parts
    count = 2 * chips * sub

    def peer_at(step):
        return lax.rem(me + step, n)

    def chip_at(step):
        return {"grp": lax.rem(chip + step + chips, chips) * 2 + core}

    barrier = pltpu.get_barrier_semaphore()
    for step in range(1, n):
        pl.semaphore_signal(
            barrier, inc=1, device_id={"cache": peer_at(step)}, device_id_type=MESH
        )
    pl.semaphore_signal(barrier, inc=1, device_id=sibling, device_id_type=MESH)
    for step in range(1, chips):
        pl.semaphore_signal(barrier, inc=1, device_id=chip_at(step), device_id_type=MESH)
    loads = [
        pltpu.make_async_copy(src, dst, w_sem.at[i])
        for i, (src, dst) in enumerate(((wo, wo_v), (wg, wg_v), (wu, wu_v), (wd, wd_v)))
    ]
    for load in loads:
        load.start()
    loads[0].wait()

    if sub % 16 == 0:
        heads_in = att[...].reshape(n * rows, att.shape[2])
    else:
        heads_in = att[...].astype(F32).reshape(n * rows, att.shape[2]).astype(BF16)
    tall = 512

    def project_tile(i, carry):
        at = pl.ds(pl.multiple_of(i * tall, tall), tall)
        y = jnp.dot(heads_in, wo_v[:, at], preferred_element_type=F32)
        z_out[:, :, :, at] = y.reshape(n, parts, sub, tall).astype(BF16)
        return carry

    lax.fori_loop(0, depth // tall, project_tile, 0)
    pl.semaphore_wait(barrier, n - 1 + 1 + chips - 1)

    def z_copy(p, step):
        return pltpu.make_async_remote_copy(
            z_out.at[peer_at(step), p], z_in.at[p, step], z_send.at[p, step], z_recv.at[p, step],
            device_id={"cache": peer_at(step)}, device_id_type=MESH,
        )

    def gather_copy(p, j):
        return pltpu.make_async_remote_copy(
            xg.at[p, 0], xg.at[p, 2 * j], a_send.at[p, j], a_recv.at[p, j],
            device_id=chip_at(j), device_id_type=MESH,
        )

    def pass_copy(p, j):
        return pltpu.make_async_remote_copy(
            xg.at[p, 2 * j], xg.at[p, 2 * j + 1], f_send.at[p, j], f_recv.at[p, j],
            device_id=sibling, device_id_type=MESH,
        )

    def sib_copy(p, j):
        return pltpu.make_async_remote_copy(
            dpart.at[p, 2 * j + 1], sib_in.at[p, j], s_send.at[p, j], s_recv.at[p, j],
            device_id=sibling, device_id_type=MESH,
        )

    def end_copy(p, j):
        return pltpu.make_async_remote_copy(
            fin_out.at[p, j], fin_in.at[p, j], e_send.at[p, j], e_recv.at[p, j],
            device_id=chip_at(-j), device_id_type=MESH,
        )

    def own(p):
        return slice(p * sub, (p + 1) * sub)

    def mix(p):
        whole = z_out[me, p].astype(F32)
        for step in range(1, n):
            z_copy(p, step).wait_recv()
            whole = whole + z_in[p, step].astype(F32)
        result = (tokens[own(p), :].astype(F32) + whole).astype(BF16)
        mixed[own(p), :] = result
        xg[p, 0] = norm(result.astype(F32), gain[...])
        for j in range(1, chips):
            gather_copy(p, j).start()
        pass_copy(p, 0).start()

    def pass_on(p):
        for j in range(1, chips):
            gather_copy(p, j).wait_recv()
            pass_copy(p, j).start()

    wide = 256

    def feed(p):
        for j in range(chips):
            pass_copy(p, j).wait_recv()
        if p == 0:
            loads[1].wait()
            loads[2].wait()
        if sub % 16 == 0:
            x = xg[p].reshape(count, depth)
        else:
            x = xg[p].astype(F32).reshape(count, depth).astype(BF16)

        def gate_tile(i, carry):
            at = pl.ds(pl.multiple_of(i * wide, wide), wide)
            gate = jnp.dot(x, wg_v[:, at], preferred_element_type=F32)
            upper = jnp.dot(x, wu_v[:, at], preferred_element_type=F32)
            units[:, at] = (gate / (1.0 + jnp.exp(-gate)) * upper).astype(BF16)
            return carry

        lax.fori_loop(0, wg_v.shape[1] // wide, gate_tile, 0)
        if p == 0:
            loads[3].wait()
        u = units[...]

        def down_tile(i, carry):
            at = pl.ds(pl.multiple_of(i * tall, tall), tall)
            y = jnp.dot(u, wd_v[:, at], preferred_element_type=F32)
            dpart[p, :, :, at] = y.reshape(2 * chips, sub, tall).astype(BF16)
            return carry

        lax.fori_loop(0, depth // tall, down_tile, 0)
        for j in range(1, chips):
            sib_copy(p, j).start()
        sib_copy(p, 0).start()

    def send_on(p):
        for j in range(1, chips):
            sib_copy(p, j).wait_recv()
            fin_out[p, j] = (dpart[p, 2 * j].astype(F32) + sib_in[p, j].astype(F32)).astype(BF16)
            end_copy(p, j).start()

    def end(p):
        sib_copy(p, 0).wait_recv()
        total = mixed[own(p), :].astype(F32) + dpart[p, 0].astype(F32) + sib_in[p, 0].astype(F32)
        for j in range(1, chips):
            end_copy(p, j).wait_recv()
            total = total + fin_in[p, j].astype(F32)
        out[own(p), :] = total.astype(BF16)

    for p in range(parts):
        for step in range(1, n):
            z_copy(p, step).start()

    mix(0)
    pass_on(0)
    for p in range(parts):
        feed(p)
        if p + 1 < parts:
            mix(p + 1)
            send_on(p)
            pass_on(p + 1)
        else:
            send_on(p)
    for p in range(parts):
        end(p)

    for p in range(parts):
        for step in range(1, n):
            z_copy(p, step).wait_send()
        for j in range(chips):
            if j > 0:
                gather_copy(p, j).wait_send()
                end_copy(p, j).wait_send()
            pass_copy(p, j).wait_send()
            sib_copy(p, j).wait_send()


def on_device(
    n, groups, tokens, attn_gain, w_query, w_key, w_value, w_out, mlp_gain, w_gate, w_up, w_down,
    key_cache, value_cache, lengths, parents, accepted,
):
    requests, heads, slots, head_dim = key_cache.shape
    tree = parents.shape[1]
    rows, depth = tokens.shape
    q_width, kv_width, ff = w_query.shape[1], w_key.shape[1], w_gate.shape[1]
    chips = groups // 2
    half = head_dim // 2
    freq = np.power(np.float32(THETA), -np.arange(half, dtype=np.float32) * np.float32(2.0 / head_dim))
    freq = jnp.asarray(np.tile(freq, 128 // half)[None, :], F32)

    vmem = pl.BlockSpec(memory_space=pltpu.VMEM)
    hbm = pl.BlockSpec(memory_space=pl.ANY)
    dma = pltpu.SemaphoreType.DMA
    query, keys, values, masks = pl.pallas_call(
        functools.partial(project_kernel, n, head_dim),
        out_shape=[
            jax.ShapeDtypeStruct((n, rows, width), BF16) for width in (q_width, kv_width, kv_width)
        ] + [jax.ShapeDtypeStruct((requests * tree, tree), F32)],
        in_specs=[pl.BlockSpec(memory_space=pltpu.SMEM)] + [vmem] * 4 + [hbm] * 3,
        out_specs=[vmem] * 4,
        scratch_shapes=[
            pltpu.VMEM((requests * tree, 128), F32),
            pltpu.VMEM((requests * tree, 128), F32),
            pltpu.VMEM((n, rows, depth), BF16),
            pltpu.VMEM(w_query.shape, BF16),
            pltpu.VMEM(w_key.shape, BF16),
            pltpu.VMEM(w_value.shape, BF16),
            dma((3,)), dma((n,)), dma((n,)), dma((n,)), dma((n,)),
        ],
        compiler_params=pltpu.CompilerParams(
            collective_id=0, has_side_effects=True, vmem_limit_bytes=VMEM_BYTES
        ),
        name="project",
    )(lengths, tokens, attn_gain.reshape(1, -1), parents, freq, w_query, w_key, w_value)

    chunk = min(512, slots)
    cache_spec = pl.BlockSpec((1, heads, head_dim, slots), lambda r, *_: (r, 0, 0, 0))
    flipped = jax.ShapeDtypeStruct((requests, heads, head_dim, slots), BF16)

    def rows_spec(width):
        return pl.BlockSpec((tree, width), lambda r, *_: (r, 0))

    attended, new_keys, new_values = pl.pallas_call(
        functools.partial(attend_kernel, heads, head_dim, chunk),
        out_shape=[jax.ShapeDtypeStruct((requests * tree, q_width), BF16), flipped, flipped],
        grid_spec=pltpu.PrefetchScalarGridSpec(
            num_scalar_prefetch=2,
            grid=(requests,),
            in_specs=[
                rows_spec(q_width), rows_spec(kv_width), rows_spec(kv_width), rows_spec(tree),
                cache_spec, cache_spec,
            ],
            out_specs=[rows_spec(q_width), cache_spec, cache_spec],
        ),
        compiler_params=pltpu.CompilerParams(vmem_limit_bytes=VMEM_BYTES),
        name="attend",
    )(
        lengths, accepted,
        query.reshape(-1, q_width), keys.reshape(-1, kv_width), values.reshape(-1, kv_width),
        masks,
        jnp.swapaxes(key_cache, 2, 3), jnp.swapaxes(value_cache, 2, 3),
    )

    parts = rows // 16 if rows % 16 == 0 else 1
    sub = rows // parts

    def blocks(count):
        return pltpu.VMEM((parts, count, sub, depth), BF16)

    hidden = pl.pallas_call(
        functools.partial(finish_kernel, n, chips, parts),
        out_shape=jax.ShapeDtypeStruct((rows, depth), BF16),
        in_specs=[vmem] * 3 + [hbm] * 4,
        out_specs=vmem,
        scratch_shapes=[
            pltpu.VMEM(w_out.shape, BF16),
            pltpu.VMEM(w_gate.shape, BF16),
            pltpu.VMEM(w_up.shape, BF16),
            pltpu.VMEM(w_down.shape, BF16),
            pltpu.VMEM((n, parts, sub, depth), BF16),
            blocks(n),
            pltpu.VMEM((rows, depth), BF16),
            blocks(2 * chips),
            pltpu.VMEM((2 * chips * sub, ff), BF16),
            blocks(2 * chips),
            blocks(chips), blocks(chips), blocks(chips),
            dma((4,)), dma((parts, n)), dma((parts, n)),
            dma((parts, chips)), dma((parts, chips)), dma((parts, chips)), dma((parts, chips)),
            dma((parts, chips)), dma((parts, chips)), dma((parts, chips)), dma((parts, chips)),
        ],
        compiler_params=pltpu.CompilerParams(
            collective_id=1, has_side_effects=True, vmem_limit_bytes=VMEM_BYTES
        ),
        name="finish",
    )(
        attended.reshape(n, rows, q_width), tokens, mlp_gain.reshape(1, -1),
        w_out, w_gate, w_up, w_down,
    )
    return (hidden, jnp.swapaxes(new_keys, 2, 3), jnp.swapaxes(new_values, 2, 3))


def solution(mesh):
    placed = (
        P(("grp", "cache"), None),
        P(),
        P(None, "cache"),
        P(None, "cache"),
        P(None, "cache"),
        P("cache", None),
        P(),
        P(None, "grp"),
        P(None, "grp"),
        P("grp", None),
        P("grp", "cache", None, None),
        P("grp", "cache", None, None),
        P("grp"),
        P("grp", None),
        P("grp", None),
    )
    return jax.shard_map(
        functools.partial(on_device, mesh.shape["cache"], mesh.shape["grp"]),
        mesh=mesh,
        in_specs=placed,
        out_specs=(
            P(("grp", "cache"), None),
            P("grp", "cache", None, None),
            P("grp", "cache", None, None),
        ),
        check_vma=False,
    )
```

```python
import functools

import jax
import jax.numpy as jnp
import numpy as np
from jax import lax
from jax.experimental import pallas as pl
from jax.experimental.pallas import tpu as pltpu
from jax.sharding import PartitionSpec as P

THETA = 10000.0
MESH = pl.DeviceIdType.MESH
F32 = jnp.float32
BF16 = jnp.bfloat16
VMEM_BYTES = 60 * 2**20


def family(parent_row, count):
    row = lax.broadcasted_iota(jnp.int32, (count, count), 0)
    lane = lax.broadcasted_iota(jnp.int32, (count, count), 1)
    linked = ((parent_row == row) & (lane > 0)) | (row == lane)
    flipped = jnp.where(linked, 1.0, 0.0).astype(BF16)
    for sweep in range((count - 1).bit_length()):
        flipped = jnp.minimum(
            jnp.dot(flipped, flipped, preferred_element_type=F32), 1.0
        ).astype(BF16)
    same = jnp.where(row == lane, 1.0, 0.0).astype(BF16)
    first = (((0,), (0,)), ((), ()))
    closure = lax.dot_general(flipped, same, first, preferred_element_type=F32)
    ones = jnp.ones((count, 128), BF16)
    depth = lax.dot_general(flipped, ones, first, preferred_element_type=F32) - 1.0
    return closure, depth


def norm(wide, gain):
    scale = lax.rsqrt(jnp.mean(wide * wide, axis=-1, keepdims=True) + 1e-05)
    return (wide * scale * gain.astype(F32).reshape(1, -1)).astype(BF16)


def turn(values, cosine, sine, head_dim):
    width = values.shape[1]
    half = head_dim // 2
    if width % 128 == 0:
        lane = lax.broadcasted_iota(jnp.int32, values.shape, 1)
        other = jnp.where(
            lane % head_dim < half,
            pltpu.roll(values, width - half, 1),
            pltpu.roll(values, half, 1),
        )
        times = width // cosine.shape[1]
        cosine = jnp.concatenate([cosine] * times, axis=1)
        sine = jnp.concatenate([sine] * times, axis=1)
    else:
        parts = []
        for at in range(0, width, head_dim):
            parts += [values[:, at + half : at + head_dim], values[:, at : at + half]]
        other = jnp.concatenate(parts, axis=1)
        cosine, sine = cosine[:, :width], sine[:, :width]
    return values * cosine + other * sine


def project_kernel(
    n, head_dim, lengths, tokens, gain, parents, freq, wq, wk, wv, q_out, k_out, v_out, mask_out,
    cosine, sine, held, wq_v, wk_v, wv_v, w_sem, left_send, left_recv, right_send, right_recv,
):
    me = lax.axis_index("cache")
    barrier = pltpu.get_barrier_semaphore()
    for step in range(1, n):
        pl.semaphore_signal(
            barrier, inc=1, device_id={"cache": lax.rem(me + step, n)}, device_id_type=MESH
        )
    loads = [
        pltpu.make_async_copy(src, dst, w_sem.at[i])
        for i, (src, dst) in enumerate(((wq, wq_v), (wk, wk_v), (wv, wv_v)))
    ]
    for load in loads:
        load.start()
    held[me] = norm(tokens[...].astype(F32), gain[...])
    pl.semaphore_wait(barrier, n - 1)

    def to_right(block):
        return pltpu.make_async_remote_copy(
            held.at[block], held.at[block], right_send.at[block], right_recv.at[block],
            device_id={"cache": lax.rem(me + 1, n)}, device_id_type=MESH,
        )

    def to_left(block):
        return pltpu.make_async_remote_copy(
            held.at[block], held.at[block], left_send.at[block], left_recv.at[block],
            device_id={"cache": lax.rem(me + n - 1, n)}, device_id_type=MESH,
        )

    rows = tokens.shape[0]

    def compute(block):
        x = held[block]
        at = pl.ds(pl.multiple_of(block * rows, 8), rows)
        cos, sin = cosine[at, :], sine[at, :]
        q_out[block] = turn(
            jnp.dot(x, wq_v[...], preferred_element_type=F32), cos, sin, head_dim
        ).astype(BF16)
        k_out[block] = turn(
            jnp.dot(x, wk_v[...], preferred_element_type=F32), cos, sin, head_dim
        ).astype(BF16)
        v_out[block] = jnp.dot(x, wv_v[...], preferred_element_type=F32).astype(BF16)

    @pl.when(me < n - 1)
    def _():
        to_right(me).start()

    @pl.when(me > 0)
    def _():
        to_left(me).start()

    requests, tree = parents.shape
    lane = lax.broadcasted_iota(jnp.int32, (tree, 128), 1)
    for r in range(requests):
        at = slice(r * tree, (r + 1) * tree)
        mask_out[at, :], depth = family(parents[r : r + 1, :], tree)
        angle = (depth + lengths[r].astype(F32)) * freq[...]
        cosine[at, :] = jnp.cos(angle)
        flat = jnp.sin(angle)
        sine[at, :] = jnp.where(lane % head_dim < head_dim // 2, -flat, flat)
    for load in loads:
        load.wait()
    compute(me)

    def hop(step, carry):
        low, high = me - step, me + step

        @pl.when(low >= 0)
        def _():
            to_right(low).wait_recv()

            @pl.when(me < n - 1)
            def _():
                to_right(low).start()

        @pl.when(high < n)
        def _():
            to_left(high).wait_recv()

            @pl.when(me > 0)
            def _():
                to_left(high).start()

        @pl.when(low >= 0)
        def _():
            compute(low)

        @pl.when(high < n)
        def _():
            compute(high)

        return carry

    lax.fori_loop(1, n, hop, 0)

    for block in range(n):
        @pl.when((block <= me) & (me < n - 1))
        def _():
            to_right(block).wait_send()

        @pl.when((block >= me) & (me > 0))
        def _():
            to_left(block).wait_send()


def attend_kernel(
    heads, head_dim, chunk, lengths, accepted, q_ref, k_ref, v_ref, mask_ref, kc, vc,
    o_ref, kc_out, vc_out,
):
    request = pl.program_id(0)
    length = lengths[request]
    slots = kc.shape[3]
    tree = q_ref.shape[0]
    group = q_ref.shape[1] // (heads * head_dim)
    factor = (head_dim ** -0.5) * 1.4426950408889634
    picks = accepted.shape[1]
    window = 256
    base = pl.multiple_of(jnp.minimum((length // 128) * 128, slots - window), 128)
    node = lax.broadcasted_iota(jnp.int32, (tree, window), 0)
    slot = lax.broadcasted_iota(jnp.int32, (tree, window), 1) + base - length
    chosen = jnp.zeros((tree, window), F32)
    for j in range(picks):
        hit = (slot == j) & (node == accepted[request, j])
        chosen = jnp.where(hit, 1.0, chosen)
    chosen = chosen.astype(BF16)
    slot_h = lax.broadcasted_iota(jnp.int32, (head_dim, window), 1) + base - length
    fresh = (slot_h >= 0) & (slot_h < picks)
    mask = jnp.concatenate([mask_ref[...]] * group, axis=0) > 0.5
    trans = (((1,), (1,)), ((), ()))
    first = (((0,), (0,)), ((), ()))

    def join(scores, values, carry, dims):
        top, total, mix = carry
        high = jnp.maximum(top, jnp.max(scores, axis=1, keepdims=True))
        shrink = jnp.exp2((top - high) * factor)
        exps = jnp.exp2((scores - high) * factor)
        total = total * shrink + jnp.sum(exps, axis=1, keepdims=True)
        mix = mix * shrink + lax.dot_general(
            exps.astype(BF16), values, dims, preferred_element_type=F32
        )
        return high, total, mix

    plain = (((1,), (0,)), ((), ()))
    queries, states = [], []
    for head in range(heads):
        at = head * group * head_dim
        query = jnp.concatenate(
            [q_ref[:, at + g * head_dim : at + (g + 1) * head_dim] for g in range(group)], axis=0
        )
        k_new = k_ref[:, head * head_dim : (head + 1) * head_dim]
        v_new = v_ref[:, head * head_dim : (head + 1) * head_dim]
        scores = lax.dot_general(query, k_new, trans, preferred_element_type=F32)
        scores = jnp.where(mask, scores, -jnp.inf)
        top = jnp.max(scores, axis=1, keepdims=True)
        exps = jnp.exp2((scores - top) * factor)
        total = jnp.sum(exps, axis=1, keepdims=True)
        mix = lax.dot_general(exps.astype(BF16), v_new, plain, preferred_element_type=F32)
        queries.append(query)
        states.append((top, total, mix))

    def part(i, carry):
        at = pl.ds(pl.multiple_of(i * chunk, chunk), chunk)
        scores = [
            jnp.dot(queries[head], kc[0, head, :, at], preferred_element_type=F32)
            for head in range(heads)
        ]
        return tuple(
            join(scores[head], vc[0, head, :, at], carry[head], trans) for head in range(heads)
        )

    full = length // chunk
    states = lax.fori_loop(0, full, part, tuple(states))
    start = pl.multiple_of(jnp.minimum(full * chunk, slots - chunk), chunk)
    at = pl.ds(start, chunk)
    where_at = lax.broadcasted_iota(jnp.int32, (1, chunk), 1) + start
    valid = (where_at < length) & (where_at >= full * chunk)
    for head in range(heads):
        scores = jnp.dot(queries[head], kc[0, head, :, at], preferred_element_type=F32)
        scores = jnp.where(valid, scores, -jnp.inf)
        top, total, mix = join(scores, vc[0, head, :, at], states[head], trans)
        out = (mix / total).astype(BF16)
        base_at = head * group * head_dim
        for g in range(group):
            o_ref[:, base_at + g * head_dim : base_at + (g + 1) * head_dim] = out[
                g * tree : (g + 1) * tree
            ]

        for cache, fed, result in ((kc, k_ref, kc_out), (vc, v_ref, vc_out)):
            new = fed[:, head * head_dim : (head + 1) * head_dim]
            result[0, head] = cache[0, head]
            placed = lax.dot_general(new, chosen, first, preferred_element_type=F32).astype(BF16)
            old = cache[0, head, :, pl.ds(base, window)]
            result[0, head, :, pl.ds(base, window)] = jnp.where(fresh, placed, old)


def finish_kernel(
    n, chips, parts, att, tokens, gain, wo, wg, wu, wd, out,
    wo_v, wg_v, wu_v, wd_v, z_out, z_in, mixed, xg, units, dpart, sib_in, fin_out, fin_in,
    w_sem, z_send, z_recv, a_send, a_recv, f_send, f_recv, s_send, s_recv, e_send, e_recv,
):
    me = lax.axis_index("cache")
    grp = lax.axis_index("grp")
    chip, core = grp // 2, lax.rem(grp, 2)
    sibling = {"grp": chip * 2 + 1 - core}
    rows, depth = tokens.shape
    sub = rows // parts
    count = 2 * chips * sub

    def peer_at(step):
        return lax.rem(me + step, n)

    def chip_at(step):
        return {"grp": lax.rem(chip + step + chips, chips) * 2 + core}

    barrier = pltpu.get_barrier_semaphore()
    for step in range(1, n):
        pl.semaphore_signal(
            barrier, inc=1, device_id={"cache": peer_at(step)}, device_id_type=MESH
        )
    pl.semaphore_signal(barrier, inc=1, device_id=sibling, device_id_type=MESH)
    for step in range(1, chips):
        pl.semaphore_signal(barrier, inc=1, device_id=chip_at(step), device_id_type=MESH)
    loads = [
        pltpu.make_async_copy(src, dst, w_sem.at[i])
        for i, (src, dst) in enumerate(((wo, wo_v), (wg, wg_v), (wu, wu_v), (wd, wd_v)))
    ]
    for load in loads:
        load.start()
    loads[0].wait()

    if sub % 16 == 0:
        heads_in = att[...].reshape(n * rows, att.shape[2])
    else:
        heads_in = att[...].astype(F32).reshape(n * rows, att.shape[2]).astype(BF16)
    tall = 512

    def project_tile(i, carry):
        at = pl.ds(pl.multiple_of(i * tall, tall), tall)
        y = jnp.dot(heads_in, wo_v[:, at], preferred_element_type=F32)
        z_out[:, :, :, at] = y.reshape(n, parts, sub, tall).astype(BF16)
        return carry

    lax.fori_loop(0, depth // tall, project_tile, 0)
    pl.semaphore_wait(barrier, n - 1 + 1 + chips - 1)

    def z_copy(p, step):
        return pltpu.make_async_remote_copy(
            z_out.at[peer_at(step), p], z_in.at[p, step], z_send.at[p, step], z_recv.at[p, step],
            device_id={"cache": peer_at(step)}, device_id_type=MESH,
        )

    def gather_copy(p, j):
        return pltpu.make_async_remote_copy(
            xg.at[p, 0], xg.at[p, 2 * j], a_send.at[p, j], a_recv.at[p, j],
            device_id=chip_at(j), device_id_type=MESH,
        )

    def pass_copy(p, j):
        return pltpu.make_async_remote_copy(
            xg.at[p, 2 * j], xg.at[p, 2 * j + 1], f_send.at[p, j], f_recv.at[p, j],
            device_id=sibling, device_id_type=MESH,
        )

    def sib_copy(p, j):
        return pltpu.make_async_remote_copy(
            dpart.at[p, 2 * j + 1], sib_in.at[p, j], s_send.at[p, j], s_recv.at[p, j],
            device_id=sibling, device_id_type=MESH,
        )

    def end_copy(p, j):
        return pltpu.make_async_remote_copy(
            fin_out.at[p, j], fin_in.at[p, j], e_send.at[p, j], e_recv.at[p, j],
            device_id=chip_at(-j), device_id_type=MESH,
        )

    def z_start(p):
        for step in range(1, n):
            z_copy(p, step).start()

    def own(p):
        return slice(p * sub, (p + 1) * sub)

    def mix(p):
        whole = z_out[me, p].astype(F32)
        for step in range(1, n):
            z_copy(p, step).wait_recv()
        if p + 1 < parts:
            z_start(p + 1)
        for step in range(1, n):
            whole = whole + z_in[p, step].astype(F32)
        result = (tokens[own(p), :].astype(F32) + whole).astype(BF16)
        mixed[own(p), :] = result
        xg[p, 0] = norm(result.astype(F32), gain[...])
        for j in range(1, chips):
            gather_copy(p, j).start()
        pass_copy(p, 0).start()

    def pass_on(p):
        for j in range(1, chips):
            gather_copy(p, j).wait_recv()
            pass_copy(p, j).start()

    wide = 256

    def feed(p):
        for j in range(chips):
            pass_copy(p, j).wait_recv()
        if p == 0:
            loads[1].wait()
            loads[2].wait()
        if sub % 16 == 0:
            x = xg[p].reshape(count, depth)
        else:
            x = xg[p].astype(F32).reshape(count, depth).astype(BF16)

        def gate_tile(i, carry):
            at = pl.ds(pl.multiple_of(i * wide, wide), wide)
            gate = jnp.dot(x, wg_v[:, at], preferred_element_type=F32)
            upper = jnp.dot(x, wu_v[:, at], preferred_element_type=F32)
            units[:, at] = (gate / (1.0 + jnp.exp(-gate)) * upper).astype(BF16)
            return carry

        lax.fori_loop(0, wg_v.shape[1] // wide, gate_tile, 0)
        if p == 0:
            loads[3].wait()
        u = units[...]

        def down_tile(i, carry):
            at = pl.ds(pl.multiple_of(i * tall, tall), tall)
            y = jnp.dot(u, wd_v[:, at], preferred_element_type=F32)
            dpart[p, :, :, at] = y.reshape(2 * chips, sub, tall).astype(BF16)
            return carry

        lax.fori_loop(0, depth // tall, down_tile, 0)
        for j in range(1, chips):
            sib_copy(p, j).start()
        sib_copy(p, 0).start()

    def send_on(p):
        for j in range(1, chips):
            sib_copy(p, j).wait_recv()
            fin_out[p, j] = (dpart[p, 2 * j].astype(F32) + sib_in[p, j].astype(F32)).astype(BF16)
            end_copy(p, j).start()

    def end(p):
        sib_copy(p, 0).wait_recv()
        total = mixed[own(p), :].astype(F32) + dpart[p, 0].astype(F32) + sib_in[p, 0].astype(F32)
        for j in range(1, chips):
            end_copy(p, j).wait_recv()
            total = total + fin_in[p, j].astype(F32)
        out[own(p), :] = total.astype(BF16)

    z_start(0)
    mix(0)
    pass_on(0)
    for p in range(parts):
        if p + 1 < parts:
            mix(p + 1)
        feed(p)
        if p + 1 < parts:
            pass_on(p + 1)
        send_on(p)
    for p in range(parts):
        end(p)

    for p in range(parts):
        for step in range(1, n):
            z_copy(p, step).wait_send()
        for j in range(chips):
            if j > 0:
                gather_copy(p, j).wait_send()
                end_copy(p, j).wait_send()
            pass_copy(p, j).wait_send()
            sib_copy(p, j).wait_send()


def on_device(
    n, groups, tokens, attn_gain, w_query, w_key, w_value, w_out, mlp_gain, w_gate, w_up, w_down,
    key_cache, value_cache, lengths, parents, accepted,
):
    requests, heads, slots, head_dim = key_cache.shape
    tree = parents.shape[1]
    rows, depth = tokens.shape
    q_width, kv_width, ff = w_query.shape[1], w_key.shape[1], w_gate.shape[1]
    chips = groups // 2
    half = head_dim // 2
    freq = np.power(np.float32(THETA), -np.arange(half, dtype=np.float32) * np.float32(2.0 / head_dim))
    freq = jnp.asarray(np.tile(freq, 128 // half)[None, :], F32)

    vmem = pl.BlockSpec(memory_space=pltpu.VMEM)
    hbm = pl.BlockSpec(memory_space=pl.ANY)
    dma = pltpu.SemaphoreType.DMA
    query, keys, values, masks = pl.pallas_call(
        functools.partial(project_kernel, n, head_dim),
        out_shape=[
            jax.ShapeDtypeStruct((n, rows, width), BF16) for width in (q_width, kv_width, kv_width)
        ] + [jax.ShapeDtypeStruct((requests * tree, tree), F32)],
        in_specs=[pl.BlockSpec(memory_space=pltpu.SMEM)] + [vmem] * 4 + [hbm] * 3,
        out_specs=[vmem] * 4,
        scratch_shapes=[
            pltpu.VMEM((requests * tree, 128), F32),
            pltpu.VMEM((requests * tree, 128), F32),
            pltpu.VMEM((n, rows, depth), BF16),
            pltpu.VMEM(w_query.shape, BF16),
            pltpu.VMEM(w_key.shape, BF16),
            pltpu.VMEM(w_value.shape, BF16),
            dma((3,)), dma((n,)), dma((n,)), dma((n,)), dma((n,)),
        ],
        compiler_params=pltpu.CompilerParams(
            collective_id=0, has_side_effects=True, vmem_limit_bytes=VMEM_BYTES
        ),
        name="project",
    )(lengths, tokens, attn_gain, parents, freq, w_query, w_key, w_value)

    chunk = min(512, slots)
    cache_spec = pl.BlockSpec((1, heads, head_dim, slots), lambda r, *_: (r, 0, 0, 0))
    flipped = jax.ShapeDtypeStruct((requests, heads, head_dim, slots), BF16)

    def rows_spec(width):
        return pl.BlockSpec((tree, width), lambda r, *_: (r, 0))

    attended, new_keys, new_values = pl.pallas_call(
        functools.partial(attend_kernel, heads, head_dim, chunk),
        out_shape=[jax.ShapeDtypeStruct((requests * tree, q_width), BF16), flipped, flipped],
        grid_spec=pltpu.PrefetchScalarGridSpec(
            num_scalar_prefetch=2,
            grid=(requests,),
            in_specs=[
                rows_spec(q_width), rows_spec(kv_width), rows_spec(kv_width), rows_spec(tree),
                cache_spec, cache_spec,
            ],
            out_specs=[rows_spec(q_width), cache_spec, cache_spec],
        ),
        compiler_params=pltpu.CompilerParams(vmem_limit_bytes=VMEM_BYTES),
        name="attend",
    )(
        lengths, accepted,
        query.reshape(-1, q_width), keys.reshape(-1, kv_width), values.reshape(-1, kv_width),
        masks,
        jnp.swapaxes(key_cache, 2, 3), jnp.swapaxes(value_cache, 2, 3),
    )

    parts = rows // 16 if rows % 16 == 0 else 1
    sub = rows // parts

    def blocks(count):
        return pltpu.VMEM((parts, count, sub, depth), BF16)

    hidden = pl.pallas_call(
        functools.partial(finish_kernel, n, chips, parts),
        out_shape=jax.ShapeDtypeStruct((rows, depth), BF16),
        in_specs=[vmem] * 3 + [hbm] * 4,
        out_specs=vmem,
        scratch_shapes=[
            pltpu.VMEM(w_out.shape, BF16),
            pltpu.VMEM(w_gate.shape, BF16),
            pltpu.VMEM(w_up.shape, BF16),
            pltpu.VMEM(w_down.shape, BF16),
            pltpu.VMEM((n, parts, sub, depth), BF16),
            blocks(n),
            pltpu.VMEM((rows, depth), BF16),
            blocks(2 * chips),
            pltpu.VMEM((2 * chips * sub, ff), BF16),
            blocks(2 * chips),
            blocks(chips), blocks(chips), blocks(chips),
            dma((4,)), dma((parts, n)), dma((parts, n)),
            dma((parts, chips)), dma((parts, chips)), dma((parts, chips)), dma((parts, chips)),
            dma((parts, chips)), dma((parts, chips)), dma((parts, chips)), dma((parts, chips)),
        ],
        compiler_params=pltpu.CompilerParams(
            collective_id=1, has_side_effects=True, vmem_limit_bytes=VMEM_BYTES
        ),
        name="finish",
    )(
        attended.reshape(n, rows, q_width), tokens, mlp_gain,
        w_out, w_gate, w_up, w_down,
    )
    return (hidden, jnp.swapaxes(new_keys, 2, 3), jnp.swapaxes(new_values, 2, 3))


def solution(mesh):
    placed = (
        P(("grp", "cache"), None),
        P(),
        P(None, "cache"),
        P(None, "cache"),
        P(None, "cache"),
        P("cache", None),
        P(),
        P(None, "grp"),
        P(None, "grp"),
        P("grp", None),
        P("grp", "cache", None, None),
        P("grp", "cache", None, None),
        P("grp"),
        P("grp", None),
        P("grp", None),
    )
    return jax.shard_map(
        functools.partial(on_device, mesh.shape["cache"], mesh.shape["grp"]),
        mesh=mesh,
        in_specs=placed,
        out_specs=(
            P(("grp", "cache"), None),
            P("grp", "cache", None, None),
            P("grp", "cache", None, None),
        ),
        check_vma=False,
    )
```
